256 devices in a mesh: group: 64 (over z_lo, y, x, core), head: 4 (over z_hi).
Axes of the slice: x: 4, y: 4, z: 8 (z_hi: 4, z_lo: 2; z = z_hi * 2 + z_lo), core: 2. Of those that a mesh axis runs over, the one named last changes fastest.
Arguments:
- queries: bfloat16 [65536, 3072], P(('group', 'head')), may hold values from -160 to 160
- keys: bfloat16 [65536, 3072], P(('group', 'head')), may hold values from -8 to 8
- values: bfloat16 [65536, 3072], P(('group', 'head')), may hold values from -6 to 6
- noise_level: int32 [64], replicated, may hold values from 0 to 7, as said below
- tile_mask: int32 [64, 8, 16], P('group'), may hold values from 0 to 1, as said below
Outputs:
- attended: bfloat16 [65536, 3072], P(('group', 'head'))
The draws below stay inside these ranges and needn't reach their ends.
Inputs may be any that keep to these rules, and one draw needn't show every extreme that they name: `tile_mask`: entries are 0 or 1; for every group, query tile i always sees key tiles i and 8 + i. `noise_level`: the first group is at level 0, the last at level 7, and the group before the last is at a lower level than the last.
All inputs are finite; a program needn't handle non-finite values.
Results may differ from the reference program's by a relative error of at most 0.0047.
Values may be sent and summed in bfloat16 or wider, within the bound.
No kernel may reach another device: no remote copies, remote signals or barrier semaphores. Data moves between devices by JAX's collectives and lax.ppermute only.
A program may use at most 128 MiB of HBM per device.

```python
import math
import jax
import jax.numpy as jnp
from jax import lax

HEADS = 24
HD = 128
TILE = 128
TOK_GROUP = 1024
TILES = 8
GROUPS = 64
TOKENS = 65536
LEVELS = 8


def base_keys(key):
    return jnp.clip(jax.random.normal(key, (TOKENS, HEADS * HD), jnp.float32), -6.0, 6.0)


def draw_keys(key, part):
    base = base_keys(key)
    return base.astype(jnp.bfloat16)


def draw_queries(key, part):
    base = base_keys(key)
    key = jax.random.fold_in(key, 5)
    return jnp.clip(jax.random.normal(jax.random.fold_in(key, 1), base.shape, jnp.float32), -6.0, 6.0).astype(jnp.bfloat16)


def draw_noise_level(key, part):
    key = jax.random.fold_in(key, 9)
    levels = jax.random.randint(key, (GROUPS,), 0, LEVELS).astype(jnp.int32)
    index = jnp.arange(GROUPS, dtype=jnp.int32)
    levels = jnp.where(index == GROUPS - 2, jnp.minimum(levels, LEVELS - 2), levels)
    levels = jnp.where(index == GROUPS - 1, LEVELS - 1, levels)
    levels = jnp.where(index == 0, 0, levels)
    return levels.astype(jnp.int32)


def draw_tile_mask(key, part):
    key = jax.random.fold_in(key, 7)
    bits = jax.random.randint(key, (GROUPS, TILES, 2 * TILES), 0, 2)
    rows = jnp.arange(TILES)[:, None]
    cols = jnp.arange(2 * TILES)[None, :]
    fixed = jnp.logical_or(cols == rows + TILES, cols == rows).astype(jnp.int32)
    return jnp.maximum(bits, fixed[None]).astype(jnp.int32)


def block_levels(rng, extent, split, low, high):
    gain, own = 1.0, jax.random.fold_in(rng, 6)
    for dim, blocks in split:
        steps = jnp.exp(jax.random.uniform(jax.random.fold_in(own, dim), (blocks,), jnp.float32, low / len(split), high / len(split)))
        gain = gain * jnp.repeat(steps, extent[dim] // blocks).reshape([-1 if axis == dim else 1 for axis in range(len(extent))])
    return gain


def bell_draw(rng, dims, scale, bound, shards=(), kind=jnp.bfloat16):
    loudness = block_levels(rng, dims, shards, -0.22, 0.18) if shards else 1.0
    entries = jax.random.normal(rng, dims, jnp.float32) * scale * loudness
    return jnp.minimum(jnp.maximum(entries, -bound), bound).astype(kind)


def setup_inputs(seed: int = 0) -> dict:
    splits = jax.random.split(jax.random.key(seed), 6)
    return {
        "queries": draw_queries(jax.random.fold_in(splits[5], 71), 0),
        "keys": draw_keys(jax.random.fold_in(splits[5], 71), 0),
        "values": bell_draw(splits[2], (TOKENS, HEADS * HD), 1.0, 6.0, ((0, 256),)),
        "noise_level": draw_noise_level(jax.random.fold_in(splits[5], 71), 0),
        "tile_mask": draw_tile_mask(jax.random.fold_in(splits[5], 71), 0),
    }


def attend_group(query_rows, key_rows, value_rows, keep_tiles):
    rows = query_rows.shape[0]
    heads = query_rows.shape[1] // HD
    query_heads = query_rows.astype(jnp.float32).reshape(rows, heads, HD)
    key_heads = key_rows.astype(jnp.float32).reshape(2 * rows, heads, HD)
    value_heads = value_rows.astype(jnp.float32).reshape(2 * rows, heads, HD)
    scores = jnp.einsum('qhd,khd->hqk', query_heads, key_heads) / math.sqrt(HD)
    shaped = scores.reshape(heads, rows // TILE, TILE, 2 * rows // TILE, TILE)
    shaped = jnp.where(keep_tiles[None, :, None, :, None] > 0, shaped, -jnp.inf)
    scores = shaped.reshape(heads, rows, 2 * rows)
    top = lax.optimization_barrier(jnp.max(scores, axis=-1, keepdims=True))
    weights = jnp.exp(scores - top)
    total = lax.optimization_barrier(jnp.sum(weights, axis=-1))
    probs = weights.astype(jnp.bfloat16).astype(jnp.float32)
    result = jnp.einsum('hqk,khd->qhd', probs, value_heads) / jnp.transpose(total)[:, :, None]
    return result.reshape(rows, heads * HD).astype(jnp.bfloat16)

def reference(queries, keys, values, noise_level, tile_mask):
    width = queries.shape[1]
    query_all = queries.reshape(GROUPS, TOK_GROUP, width)
    key_all = keys.reshape(GROUPS, TOK_GROUP, width)
    value_all = values.reshape(GROUPS, TOK_GROUP, width)
    empty = jnp.zeros((1, TOK_GROUP, width), jnp.bfloat16)
    key_prev = jnp.concatenate([empty, key_all[:-1]], axis=0)
    value_prev = jnp.concatenate([empty, value_all[:-1]], axis=0)
    see_all = jnp.concatenate([jnp.zeros((1,), jnp.int32), (noise_level[:-1] < noise_level[1:]).astype(jnp.int32)])

    def one_group(items):
        query_rows, key_rows, value_rows, key_old, value_old, mask_rows, see = items
        gate = jnp.concatenate([jnp.full((TILES,), see, jnp.int32), jnp.ones((TILES,), jnp.int32)])
        keep_tiles = mask_rows * gate[None, :]
        context_keys = jnp.concatenate([key_old, key_rows], axis=0)
        context_values = jnp.concatenate([value_old, value_rows], axis=0)
        return attend_group(query_rows, context_keys, context_values, keep_tiles)
    result = lax.map(one_group, (query_all, key_all, value_all, key_prev, value_prev, tile_mask, see_all))
    return result.reshape(TOKENS, width)
```

```python
import functools
import math

import jax
import jax.numpy as jnp
from jax import lax
from jax.experimental import pallas as pl
from jax.experimental.pallas import tpu as pltpu
from jax.sharding import PartitionSpec as P

HD = 128
TILE = 128
CHUNKS = ((2, 1), (2, 0), (2, 1))
SCALE = math.log2(math.e) / math.sqrt(HD)
ANY = pl.BlockSpec(memory_space=pl.ANY)
SMEM = pl.BlockSpec(memory_space=pltpu.SMEM)
BUSY = 1 << 36
VMEM_LIMIT = 60 * 1024 * 1024


def run_copies(pairs, stage, sems):
    count = len(pairs)
    slots = [stage.at[i] for i in range(count)]
    reads = [
        pltpu.make_async_copy(pairs[i][0], slots[i], sems.at[0, i]) for i in range(count)
    ]
    writes = [
        pltpu.make_async_copy(slots[i], pairs[i][1], sems.at[1, i]) for i in range(count)
    ]
    for read in reads:
        read.start()
    for read, write in zip(reads, writes):
        read.wait()
        write.start()
    for write in writes:
        write.wait()


def staging(count, shape):
    return [pltpu.VMEM((count, *shape), jnp.bfloat16), pltpu.SemaphoreType.DMA((2, count))]


def column(block, ways, width, start):
    return pl.multiple_of(lax.rem(block, ways) * (width // ways) + start, HD)


def turned(chunk):
    group, count = lax.axis_index("group"), lax.axis_size("group")
    return jnp.where(group >= count // 2, jnp.int32(chunk[1]), jnp.int32(0))


def spans():
    start = 0
    for chunk in CHUNKS:
        yield chunk, start * HD, chunk[0] * HD
        start += chunk[0]


def pack_body(ways, width, order, *refs):
    sources, outs, stages, sems = refs[:3], refs[3:-4], refs[-4:-1], refs[-1]
    me = lax.axis_index("head")
    block = width // ways
    copies = []
    count = len(order)
    parts = len(CHUNKS)
    for j, (chunk, start, wide) in enumerate(spans()):
        for source in (1, 2):
            for i, s in enumerate(order):
                cols = pl.ds(column(me + s + turned(chunk), ways, width, start), wide)
                slot = stages[source].at[:, pl.ds(i * block + start, wide)]
                out = outs[j * count + i].at[source - 1]
                copies.append((sources[source].at[:, cols], slot, out))
    for i, s in enumerate(order):
        for chunk, start, wide in spans():
            cols = pl.ds(column(me + s + turned(chunk), ways, width, start), wide)
            slot = stages[0].at[:, pl.ds(i * block + start, wide)]
            out = outs[parts * count + i].at[:, pl.ds(start, wide)]
            copies.append((sources[0].at[:, cols], slot, out))
    reads = [pltpu.make_async_copy(c[0], c[1], sems.at[0, i]) for i, c in enumerate(copies)]
    writes = [pltpu.make_async_copy(c[1], c[2], sems.at[1, i]) for i, c in enumerate(copies)]
    for read in reads:
        read.start()
    for read, write in zip(reads, writes):
        read.wait()
        write.start()
    for write in writes:
        write.wait()


def pack(queries, keys, values, ways, order):
    rows, width = queries.shape
    block = width // ways
    kind = queries.dtype
    shapes = []
    for _, _, wide in spans():
        shapes += [jax.ShapeDtypeStruct((2, rows, wide), kind)] * len(order)
    shapes += [jax.ShapeDtypeStruct((rows, block), kind)] * len(order)
    return pl.pallas_call(
        functools.partial(pack_body, ways, width, order),
        out_shape=shapes,
        in_specs=[ANY] * 3,
        out_specs=[ANY] * len(shapes),
        scratch_shapes=[pltpu.VMEM((rows, width), kind)] * 3
        + [pltpu.SemaphoreType.DMA((2, 3 * len(order) * len(CHUNKS)))],
        compiler_params=pltpu.CompilerParams(vmem_limit_bytes=VMEM_LIMIT),
        name="pack",
    )(queries, keys, values)


def gather_body(ways, *refs):
    pieces, out, stage, sems = refs[:ways], refs[-3], refs[-2], refs[-1]
    run_copies([(pieces[r], out.at[pl.ds(2 * r, 2)]) for r in range(ways)], stage, sems)


def gather(pieces, gates):
    ways = len(pieces)
    _, rows, wide = pieces[0].shape
    return pl.pallas_call(
        functools.partial(gather_body, ways),
        out_shape=jax.ShapeDtypeStruct((2 * ways, rows, wide), pieces[0].dtype),
        in_specs=[ANY] * (ways + len(gates)),
        out_specs=ANY,
        scratch_shapes=staging(ways, (2, rows, wide)),
        compiler_params=pltpu.CompilerParams(vmem_limit_bytes=VMEM_LIMIT),
        name="gather",
    )(*pieces, *gates)


def touch_body(*refs):
    refs[-1][0] = jnp.int32(0)


def touch(arrays):
    return pl.pallas_call(
        touch_body,
        out_shape=jax.ShapeDtypeStruct((1,), jnp.int32),
        in_specs=[ANY] * len(arrays),
        out_specs=SMEM,
        cost_estimate=pl.CostEstimate(flops=BUSY, bytes_accessed=0, transcendentals=0),
        name="touch",
    )(*arrays)


def attend_body(ways, chunk, noise, mask, *refs):
    pieces, asks, prior, outs = refs[:ways], refs[ways : 2 * ways], refs[2 * ways], refs[-ways:]
    rows = prior.shape[1]
    per = rows // TILE
    tiles = ways * per
    me, group = lax.axis_index("head"), lax.axis_index("group")
    half = lax.axis_size("group") // 2
    see = jnp.logical_and(group > 0, noise[jnp.maximum(group - 1, 0)] < noise[group])
    see = see.astype(jnp.int32)
    moved = jnp.where(group == half, turned(chunk), 0)
    first = [lax.rem(me + ways - r, ways) * per for r in range(ways)]
    before = [lax.rem(me + moved + ways - r, ways) * per for r in range(ways)]
    lane = lax.broadcasted_iota(jnp.int32, (1, rows), 1) // TILE
    context = [(prior.at[2 * p], prior.at[2 * p + 1], before[p], see) for p in range(ways)]
    context += [(pieces[p].at[0], pieces[p].at[1], tiles + first[p], 1) for p in range(ways)]

    def score(r):
        query = asks[r][...]
        scores = []
        for key, _, tile, seen in context:
            s = lax.dot_general(
                query, key[...], (((1,), (1,)), ((), ())), preferred_element_type=jnp.float32
            )
            bands = []
            for a in range(per):
                bias = jnp.full((1, rows), -jnp.inf, jnp.float32)
                for b in range(per):
                    allowed = mask[0, first[r] + a, tile + b] * seen
                    bias = jnp.where(
                        lane == b, jnp.where(allowed > 0, jnp.float32(0), -jnp.inf), bias
                    )
                bands.append(s[a * TILE : (a + 1) * TILE] + bias)
            scores.append(jnp.concatenate(bands, axis=0))
        return scores

    later = score(0)
    for r in range(ways):
        scores = later
        if r + 1 < ways:
            later = score(r + 1)
        top = functools.reduce(jnp.maximum, scores)
        top = jnp.max(top, axis=1, keepdims=True)
        total = jnp.zeros((rows, rows), jnp.float32)
        result = jnp.zeros((rows, HD), jnp.float32)
        for s, (_, value, _, _) in zip(scores, context):
            weights = jnp.exp2((s - top) * SCALE)
            total = total + weights
            result = result + jnp.dot(
                weights.astype(jnp.bfloat16), value[...], preferred_element_type=jnp.float32
            )
        total = jnp.sum(total, axis=1, keepdims=True)
        outs[r][...] = (result / total).astype(jnp.bfloat16)


def attend(noise_level, tile_mask, pieces, asks, prior, chunk, start, gates):
    ways = len(pieces)
    rows, wide = prior.shape[1:]
    heads, skip = wide // HD, start // HD
    pairs = heads * ways * rows * 2 * ways * rows
    return pl.pallas_call(
        functools.partial(attend_body, ways, chunk),
        grid=(heads,),
        out_shape=[jax.ShapeDtypeStruct((rows, wide), jnp.bfloat16)] * ways,
        in_specs=[SMEM, SMEM]
        + [pl.BlockSpec((2, rows, HD), lambda h: (0, 0, h))] * ways
        + [pl.BlockSpec((rows, HD), lambda h: (0, h + skip))] * ways
        + [pl.BlockSpec((2 * ways, rows, HD), lambda h: (0, 0, h))]
        + [ANY] * len(gates),
        out_specs=[pl.BlockSpec((rows, HD), lambda h: (0, h))] * ways,
        compiler_params=pltpu.CompilerParams(vmem_limit_bytes=VMEM_LIMIT),
        cost_estimate=pl.CostEstimate(
            flops=8 * pairs * HD, bytes_accessed=12 * ways * rows * wide, transcendentals=pairs
        ),
        name="attend",
    )(noise_level, tile_mask, *pieces, *asks, prior, *gates)


def place_body(ways, width, chunk, start, *refs):
    pieces, out, stage, sems = refs[:ways], refs[-3], refs[-2], refs[-1]
    wide = pieces[0].shape[1]
    me = lax.axis_index("head")
    run_copies(
        [
            (pieces[r], out.at[:, pl.ds(column(me + r + turned(chunk), ways, width, start), wide)])
            for r in range(ways)
        ],
        stage,
        sems,
    )


def place(pieces, width, chunk, start, earlier):
    ways = len(pieces)
    rows = pieces[0].shape[0]
    extra = [] if earlier is None else [earlier]
    return pl.pallas_call(
        functools.partial(place_body, ways, width, chunk, start),
        out_shape=jax.ShapeDtypeStruct((rows, width), pieces[0].dtype),
        in_specs=[ANY] * (ways + len(extra)),
        out_specs=ANY,
        scratch_shapes=staging(ways, pieces[0].shape),
        input_output_aliases={ways: 0} if extra else {},
        compiler_params=pltpu.CompilerParams(vmem_limit_bytes=VMEM_LIMIT),
        name="place",
    )(*pieces, *extra)


def turn(block, distance):
    if distance == 0:
        return block
    ways = lax.axis_size("head")
    return lax.ppermute(block, "head", [(i, (i + distance) % ways) for i in range(ways)])


def onward(block, chunk):
    count, ways = lax.axis_size("group"), lax.axis_size("head")
    pairs = []
    for group in range(count - 1):
        back = chunk[1] if group + 1 == count // 2 else 0
        for i in range(ways):
            pairs.append((group * ways + i, (group + 1) * ways + (i - back) % ways))
    return lax.ppermute(block, ("group", "head"), pairs)


def shards(queries, keys, values, noise_level, tile_mask):
    ways = lax.axis_size("head")
    width = queries.shape[1]
    order = (2, 1, 3, 0)
    packed = pack(queries, keys, values, ways, order)
    moved = [turn(block, order[i % ways]) for i, block in enumerate(packed)]
    parts = [
        [moved[i * ways + order.index(r)] for r in range(ways)] for i in range(1 + len(CHUNKS))
    ]
    pieces, asks = parts[:-1], parts[-1]
    gathered = []
    for part in pieces:
        gathered.append(gather(part, gathered[-1:]))
    priors = [onward(block, chunk) for block, chunk in zip(gathered, CHUNKS)]
    gates = [touch(asks)]
    out = None
    for j, (chunk, start, _) in enumerate(spans()):
        result = attend(noise_level, tile_mask, pieces[j], asks, priors[j], chunk, start, gates)
        back = [result[0]] + [turn(result[r], ways - r) for r in range(1, ways)]
        out = place(back, width, chunk, start, out)
    return out


def solution(mesh):
    split = P(("group", "head"), None)
    in_specs = (split, split, split, P(), P("group", None, None))
    return jax.shard_map(shards, mesh=mesh, in_specs=in_specs, out_specs=split, check_vma=False)
```

```python
import functools
import math

import jax
import jax.numpy as jnp
from jax import lax
from jax.experimental import pallas as pl
from jax.experimental.pallas import tpu as pltpu
from jax.sharding import PartitionSpec as P

HD = 128
TILE = 128
CHUNKS = ((3, 0), (3, 0))
RELAYED = 1
SCALE = math.log2(math.e) / math.sqrt(HD)
ANY = pl.BlockSpec(memory_space=pl.ANY)
SMEM = pl.BlockSpec(memory_space=pltpu.SMEM)
BUSY = 1 << 36
VMEM_LIMIT = 60 * 1024 * 1024


def run_copies(pairs, stage, sems):
    count = len(pairs)
    slots = [stage.at[i] for i in range(count)]
    reads = [
        pltpu.make_async_copy(pairs[i][0], slots[i], sems.at[0, i]) for i in range(count)
    ]
    writes = [
        pltpu.make_async_copy(slots[i], pairs[i][1], sems.at[1, i]) for i in range(count)
    ]
    for read in reads:
        read.start()
    for read, write in zip(reads, writes):
        read.wait()
        write.start()
    for write in writes:
        write.wait()


def staging(count, shape):
    return [pltpu.VMEM((count, *shape), jnp.bfloat16), pltpu.SemaphoreType.DMA((2, count))]


def column(block, ways, width, start):
    return pl.multiple_of(lax.rem(block, ways) * (width // ways) + start, HD)


def turned(chunk):
    group, count = lax.axis_index("group"), lax.axis_size("group")
    return jnp.where(group >= count // 2, jnp.int32(chunk[1]), jnp.int32(0))


def spans():
    start = 0
    for chunk in CHUNKS:
        yield chunk, start * HD, chunk[0] * HD
        start += chunk[0]


def pack_body(ways, width, order, *refs):
    sources, outs, stages, sems = refs[:3], refs[3:-4], refs[-4:-1], refs[-1]
    me = lax.axis_index("head")
    block = width // ways
    copies = []
    count = len(order)
    parts = len(CHUNKS)
    for j, (chunk, start, wide) in enumerate(spans()):
        for source in (1, 2):
            for i, s in enumerate(order):
                cols = pl.ds(column(me + s + turned(chunk), ways, width, start), wide)
                slot = stages[source].at[:, pl.ds(i * block + start, wide)]
                out = outs[j * count + i].at[source - 1]
                copies.append((sources[source].at[:, cols], slot, out))
    for i, s in enumerate(order):
        for chunk, start, wide in spans():
            cols = pl.ds(column(me + s + turned(chunk), ways, width, start), wide)
            slot = stages[0].at[:, pl.ds(i * block + start, wide)]
            out = outs[parts * count + i].at[:, pl.ds(start, wide)]
            copies.append((sources[0].at[:, cols], slot, out))
    reads = [pltpu.make_async_copy(c[0], c[1], sems.at[0, i]) for i, c in enumerate(copies)]
    writes = [pltpu.make_async_copy(c[1], c[2], sems.at[1, i]) for i, c in enumerate(copies)]
    for read in reads:
        read.start()
    for read, write in zip(reads, writes):
        read.wait()
        write.start()
    for write in writes:
        write.wait()


def pack(queries, keys, values, ways, order):
    rows, width = queries.shape
    block = width // ways
    kind = queries.dtype
    shapes = []
    for _, _, wide in spans():
        shapes += [jax.ShapeDtypeStruct((2, rows, wide), kind)] * len(order)
    shapes += [jax.ShapeDtypeStruct((rows, block), kind)] * len(order)
    return pl.pallas_call(
        functools.partial(pack_body, ways, width, order),
        out_shape=shapes,
        in_specs=[ANY] * 3,
        out_specs=[ANY] * len(shapes),
        scratch_shapes=[pltpu.VMEM((rows, width), kind)] * 3
        + [pltpu.SemaphoreType.DMA((2, 3 * len(order) * len(CHUNKS)))],
        compiler_params=pltpu.CompilerParams(vmem_limit_bytes=VMEM_LIMIT),
        name="pack",
    )(queries, keys, values)


def gather_body(ways, *refs):
    pieces, out, stage, sems = refs[:ways], refs[-3], refs[-2], refs[-1]
    run_copies([(pieces[r], out.at[pl.ds(2 * r, 2)]) for r in range(ways)], stage, sems)


def gather(pieces, gates):
    ways = len(pieces)
    _, rows, wide = pieces[0].shape
    return pl.pallas_call(
        functools.partial(gather_body, ways),
        out_shape=jax.ShapeDtypeStruct((2 * ways, rows, wide), pieces[0].dtype),
        in_specs=[ANY] * (ways + len(gates)),
        out_specs=ANY,
        scratch_shapes=staging(ways, (2, rows, wide)),
        compiler_params=pltpu.CompilerParams(vmem_limit_bytes=VMEM_LIMIT),
        name="gather",
    )(*pieces, *gates)


def touch_body(*refs):
    refs[-1][0] = jnp.int32(0)


def touch(arrays):
    return pl.pallas_call(
        touch_body,
        out_shape=jax.ShapeDtypeStruct((1,), jnp.int32),
        in_specs=[ANY] * len(arrays),
        out_specs=SMEM,
        cost_estimate=pl.CostEstimate(flops=BUSY, bytes_accessed=0, transcendentals=0),
        name="touch",
    )(*arrays)


def attend_body(ways, chunk, sums, noise, mask, *refs):
    pieces, asks, outs = refs[:ways], refs[ways : 2 * ways], refs[-ways:]
    priors = refs[2 * ways : 2 * ways + sums]
    rows = priors[0].shape[1]
    per = rows // TILE
    tiles = ways * per
    me, group = lax.axis_index("head"), lax.axis_index("group")
    half = lax.axis_size("group") // 2
    see = jnp.logical_and(group > 0, noise[jnp.maximum(group - 1, 0)] < noise[group])
    see = see.astype(jnp.int32)
    moved = jnp.where(group == half, turned(chunk), 0)
    first = [lax.rem(me + ways - r, ways) * per for r in range(ways)]
    before = [lax.rem(me + moved + ways - r, ways) * per for r in range(ways)]
    lane = lax.broadcasted_iota(jnp.int32, (1, rows), 1) // TILE
    past = [functools.reduce(jnp.add, [prior[i] for prior in priors]) for i in range(2 * ways)]
    context = [(past[2 * p], past[2 * p + 1], before[p], see) for p in range(ways)]
    context += [(pieces[p][0], pieces[p][1], tiles + first[p], 1) for p in range(ways)]

    def score(r):
        query = asks[r][...]
        scores = []
        for key, _, tile, seen in context:
            s = lax.dot_general(
                query, key, (((1,), (1,)), ((), ())), preferred_element_type=jnp.float32
            )
            bands = []
            for a in range(per):
                bias = jnp.full((1, rows), -jnp.inf, jnp.float32)
                for b in range(per):
                    allowed = mask[0, first[r] + a, tile + b] * seen
                    bias = jnp.where(
                        lane == b, jnp.where(allowed > 0, jnp.float32(0), -jnp.inf), bias
                    )
                bands.append(s[a * TILE : (a + 1) * TILE] + bias)
            scores.append(jnp.concatenate(bands, axis=0))
        return scores

    later = score(0)
    for r in range(ways):
        scores = later
        if r + 1 < ways:
            later = score(r + 1)
        top = functools.reduce(jnp.maximum, scores)
        top = jnp.max(top, axis=1, keepdims=True)
        total = jnp.zeros((rows, rows), jnp.float32)
        result = jnp.zeros((rows, HD), jnp.float32)
        for s, (_, value, _, _) in zip(scores, context):
            weights = jnp.exp2((s - top) * SCALE)
            total = total + weights
            result = result + jnp.dot(
                weights.astype(jnp.bfloat16), value, preferred_element_type=jnp.float32
            )
        total = jnp.sum(total, axis=1, keepdims=True)
        outs[r][...] = (result / total).astype(jnp.bfloat16)


def attend(noise_level, tile_mask, pieces, asks, priors, chunk, start, gates):
    ways = len(pieces)
    rows, wide = priors[0].shape[1:]
    heads, skip = wide // HD, start // HD
    pairs = heads * ways * rows * 2 * ways * rows
    return pl.pallas_call(
        functools.partial(attend_body, ways, chunk, len(priors)),
        grid=(heads,),
        out_shape=[jax.ShapeDtypeStruct((rows, wide), jnp.bfloat16)] * ways,
        in_specs=[SMEM, SMEM]
        + [pl.BlockSpec((2, rows, HD), lambda h: (0, 0, h))] * ways
        + [pl.BlockSpec((rows, HD), lambda h: (0, h + skip))] * ways
        + [pl.BlockSpec((2 * ways, rows, HD), lambda h: (0, 0, h))] * len(priors)
        + [ANY] * len(gates),
        out_specs=[pl.BlockSpec((rows, HD), lambda h: (0, h))] * ways,
        compiler_params=pltpu.CompilerParams(vmem_limit_bytes=VMEM_LIMIT),
        cost_estimate=pl.CostEstimate(
            flops=8 * pairs * HD, bytes_accessed=12 * ways * rows * wide, transcendentals=pairs
        ),
        name="attend",
    )(noise_level, tile_mask, *pieces, *asks, *priors, *gates)


def place_body(ways, width, chunk, start, *refs):
    pieces, out, stage, sems = refs[:ways], refs[-3], refs[-2], refs[-1]
    wide = pieces[0].shape[1]
    me = lax.axis_index("head")
    run_copies(
        [
            (pieces[r], out.at[:, pl.ds(column(me + r + turned(chunk), ways, width, start), wide)])
            for r in range(ways)
        ],
        stage,
        sems,
    )


def place(pieces, width, chunk, start, earlier):
    ways = len(pieces)
    rows = pieces[0].shape[0]
    extra = [] if earlier is None else [earlier]
    return pl.pallas_call(
        functools.partial(place_body, ways, width, chunk, start),
        out_shape=jax.ShapeDtypeStruct((rows, width), pieces[0].dtype),
        in_specs=[ANY] * (ways + len(extra)),
        out_specs=ANY,
        scratch_shapes=staging(ways, pieces[0].shape),
        input_output_aliases={ways: 0} if extra else {},
        compiler_params=pltpu.CompilerParams(vmem_limit_bytes=VMEM_LIMIT),
        name="place",
    )(*pieces, *extra)


def turn(block, distance):
    if distance == 0:
        return block
    ways = lax.axis_size("head")
    return lax.ppermute(block, "head", [(i, (i + distance) % ways) for i in range(ways)])


def onward(block, chunk, relayed):
    count, ways = lax.axis_size("group"), lax.axis_size("head")
    half = count // 2
    pairs, last = [], []
    for group in range(count - 1):
        for i in range(ways):
            there = (group + 1) * ways + i
            if group + 1 == half:
                there = half * ways + (i - chunk[1]) % ways
                if relayed:
                    last.append((i, there))
                    there = i
            pairs.append((group * ways + i, there))
    block = lax.ppermute(block, ("group", "head"), pairs)
    if not relayed:
        return [block]
    return [block, lax.ppermute(block, ("group", "head"), last)]


def shards(queries, keys, values, noise_level, tile_mask):
    ways = lax.axis_size("head")
    width = queries.shape[1]
    order = (2, 1, 3, 0)
    packed = pack(queries, keys, values, ways, order)
    moved = [turn(block, order[i % ways]) for i, block in enumerate(packed)]
    parts = [
        [moved[i * ways + order.index(r)] for r in range(ways)] for i in range(1 + len(CHUNKS))
    ]
    pieces, asks = parts[:-1], parts[-1]
    gathered = []
    for part in pieces:
        gathered.append(gather(part, gathered[-1:]))
    priors = [
        onward(block, chunk, j < RELAYED) for j, (block, chunk) in enumerate(zip(gathered, CHUNKS))
    ]
    gates = [touch([prior[0] for prior in priors[RELAYED:]])]
    out = None
    for j, (chunk, start, _) in enumerate(spans()):
        result = attend(noise_level, tile_mask, pieces[j], asks, priors[j], chunk, start, gates)
        back = [result[0]] + [turn(result[r], ways - r) for r in range(1, ways)]
        out = place(back, width, chunk, start, out)
    return out


def solution(mesh):
    split = P(("group", "head"), None)
    in_specs = (split, split, split, P(), P("group", None, None))
    return jax.shard_map(shards, mesh=mesh, in_specs=in_specs, out_specs=split, check_vma=False)
```

```python
import functools
import math

import jax
import jax.numpy as jnp
from jax import lax
from jax.experimental import pallas as pl
from jax.experimental.pallas import tpu as pltpu
from jax.sharding import PartitionSpec as P

HD = 128
TILE = 128
CHUNKS = ((3, 0), (3, 0))
RELAYED = 1
SCALE = math.log2(math.e) / math.sqrt(HD)
ANY = pl.BlockSpec(memory_space=pl.ANY)
SMEM = pl.BlockSpec(memory_space=pltpu.SMEM)
BUSY = 1 << 36
VMEM_LIMIT = 60 * 1024 * 1024


def run_copies(pairs, stage, sems):
    count = len(pairs)
    slots = [stage.at[i] for i in range(count)]
    reads = [
        pltpu.make_async_copy(pairs[i][0], slots[i], sems.at[0, i]) for i in range(count)
    ]
    writes = [
        pltpu.make_async_copy(slots[i], pairs[i][1], sems.at[1, i]) for i in range(count)
    ]
    for read in reads:
        read.start()
    for read, write in zip(reads, writes):
        read.wait()
        write.start()
    for write in writes:
        write.wait()


def staging(count, shape):
    return [pltpu.VMEM((count, *shape), jnp.bfloat16), pltpu.SemaphoreType.DMA((2, count))]


def column(block, ways, width, start):
    return pl.multiple_of(lax.rem(block, ways) * (width // ways) + start, HD)


def turned(chunk):
    group, count = lax.axis_index("group"), lax.axis_size("group")
    return jnp.where(group >= count // 2, jnp.int32(chunk[1]), jnp.int32(0))


def spans():
    start = 0
    for chunk in CHUNKS:
        yield chunk, start * HD, chunk[0] * HD
        start += chunk[0]


def pack_body(ways, width, order, *refs):
    sources, outs, stages, sems = refs[:3], refs[3:-4], refs[-4:-1], refs[-1]
    me = lax.axis_index("head")
    block = width // ways
    copies = []
    count = len(order)
    parts = len(CHUNKS)
    for j, (chunk, start, wide) in enumerate(spans()):
        for source in (1, 2):
            for i, s in enumerate(order):
                cols = pl.ds(column(me + s + turned(chunk), ways, width, start), wide)
                slot = stages[source].at[:, pl.ds(i * block + start, wide)]
                out = outs[j * count + i].at[source - 1]
                copies.append((sources[source].at[:, cols], slot, out))
    for i, s in enumerate(order):
        for chunk, start, wide in spans():
            cols = pl.ds(column(me + s + turned(chunk), ways, width, start), wide)
            slot = stages[0].at[:, pl.ds(i * block + start, wide)]
            out = outs[parts * count + i].at[:, pl.ds(start, wide)]
            copies.append((sources[0].at[:, cols], slot, out))
    reads = [pltpu.make_async_copy(c[0], c[1], sems.at[0, i]) for i, c in enumerate(copies)]
    writes = [pltpu.make_async_copy(c[1], c[2], sems.at[1, i]) for i, c in enumerate(copies)]
    for read in reads:
        read.start()
    for read, write in zip(reads, writes):
        read.wait()
        write.start()
    for write in writes:
        write.wait()


def pack(queries, keys, values, ways, order):
    rows, width = queries.shape
    block = width // ways
    kind = queries.dtype
    shapes = []
    for _, _, wide in spans():
        shapes += [jax.ShapeDtypeStruct((2, rows, wide), kind)] * len(order)
    shapes += [jax.ShapeDtypeStruct((rows, block), kind)] * len(order)
    return pl.pallas_call(
        functools.partial(pack_body, ways, width, order),
        out_shape=shapes,
        in_specs=[ANY] * 3,
        out_specs=[ANY] * len(shapes),
        scratch_shapes=[pltpu.VMEM((rows, width), kind)] * 3
        + [pltpu.SemaphoreType.DMA((2, 3 * len(order) * len(CHUNKS)))],
        compiler_params=pltpu.CompilerParams(vmem_limit_bytes=VMEM_LIMIT),
        name="pack",
    )(queries, keys, values)


def gather_body(ways, *refs):
    pieces, out, stage, sems = refs[:ways], refs[-3], refs[-2], refs[-1]
    run_copies([(pieces[r], out.at[pl.ds(2 * r, 2)]) for r in range(ways)], stage, sems)


def gather(pieces, gates):
    ways = len(pieces)
    _, rows, wide = pieces[0].shape
    return pl.pallas_call(
        functools.partial(gather_body, ways),
        out_shape=jax.ShapeDtypeStruct((2 * ways, rows, wide), pieces[0].dtype),
        in_specs=[ANY] * (ways + len(gates)),
        out_specs=ANY,
        scratch_shapes=staging(ways, (2, rows, wide)),
        compiler_params=pltpu.CompilerParams(vmem_limit_bytes=VMEM_LIMIT),
        name="gather",
    )(*pieces, *gates)


def touch_body(*refs):
    refs[-1][0] = jnp.int32(0)


def touch(arrays):
    return pl.pallas_call(
        touch_body,
        out_shape=jax.ShapeDtypeStruct((1,), jnp.int32),
        in_specs=[ANY] * len(arrays),
        out_specs=SMEM,
        cost_estimate=pl.CostEstimate(flops=BUSY, bytes_accessed=0, transcendentals=0),
        name="touch",
    )(*arrays)


def attend_body(ways, chunk, sums, noise, mask, *refs):
    pieces, asks, outs = refs[:ways], refs[ways : 2 * ways], refs[-ways:]
    priors = refs[2 * ways : 2 * ways + sums]
    rows = priors[0].shape[1]
    per = rows // TILE
    tiles = ways * per
    me, group = lax.axis_index("head"), lax.axis_index("group")
    half = lax.axis_size("group") // 2
    see = jnp.logical_and(group > 0, noise[jnp.maximum(group - 1, 0)] < noise[group])
    see = see.astype(jnp.int32)
    moved = jnp.where(group == half, turned(chunk), 0)
    first = [lax.rem(me + ways - r, ways) * per for r in range(ways)]
    before = [lax.rem(me + moved + ways - r, ways) * per for r in range(ways)]
    lane = lax.broadcasted_iota(jnp.int32, (1, rows), 1) // TILE
    past = [functools.reduce(jnp.add, [prior[i] for prior in priors]) for i in range(2 * ways)]
    context = [(past[2 * p], past[2 * p + 1], before[p], see) for p in range(ways)]
    context += [(pieces[p][0], pieces[p][1], tiles + first[p], 1) for p in range(ways)]

    def score(r):
        query = asks[r][...]
        scores = []
        for key, _, tile, seen in context:
            s = lax.dot_general(
                query, key, (((1,), (1,)), ((), ())), preferred_element_type=jnp.float32
            )
            bands = []
            for a in range(per):
                bias = jnp.full((1, rows), -jnp.inf, jnp.float32)
                for b in range(per):
                    allowed = mask[0, first[r] + a, tile + b] * seen
                    bias = jnp.where(
                        lane == b, jnp.where(allowed > 0, jnp.float32(0), -jnp.inf), bias
                    )
                bands.append(s[a * TILE : (a + 1) * TILE] + bias)
            scores.append(jnp.concatenate(bands, axis=0))
        return scores

    later = score(0)
    for r in range(ways):
        scores = later
        if r + 1 < ways:
            later = score(r + 1)
        top = functools.reduce(jnp.maximum, scores)
        top = jnp.max(top, axis=1, keepdims=True)
        total = jnp.zeros((rows, rows), jnp.float32)
        result = jnp.zeros((rows, HD), jnp.float32)
        for s, (_, value, _, _) in zip(scores, context):
            weights = jnp.exp2((s - top) * SCALE)
            total = total + weights
            result = result + jnp.dot(
                weights.astype(jnp.bfloat16), value, preferred_element_type=jnp.float32
            )
        total = jnp.sum(total, axis=1, keepdims=True)
        outs[r][...] = (result / total).astype(jnp.bfloat16)


def attend(noise_level, tile_mask, pieces, asks, priors, chunk, start, gates):
    ways = len(pieces)
    rows, wide = priors[0].shape[1:]
    heads, skip = wide // HD, start // HD
    pairs = heads * ways * rows * 2 * ways * rows
    return pl.pallas_call(
        functools.partial(attend_body, ways, chunk, len(priors)),
        grid=(heads,),
        out_shape=[jax.ShapeDtypeStruct((rows, wide), jnp.bfloat16)] * ways,
        in_specs=[SMEM, SMEM]
        + [pl.BlockSpec((2, rows, HD), lambda h: (0, 0, h))] * ways
        + [pl.BlockSpec((rows, HD), lambda h: (0, h + skip))] * ways
        + [pl.BlockSpec((2 * ways, rows, HD), lambda h: (0, 0, h))] * len(priors)
        + [ANY] * len(gates),
        out_specs=[pl.BlockSpec((rows, HD), lambda h: (0, h))] * ways,
        compiler_params=pltpu.CompilerParams(vmem_limit_bytes=VMEM_LIMIT),
        cost_estimate=pl.CostEstimate(
            flops=8 * pairs * HD, bytes_accessed=12 * ways * rows * wide, transcendentals=pairs
        ),
        name="attend",
    )(noise_level, tile_mask, *pieces, *asks, *priors, *gates)


def place_body(ways, width, chunk, start, *refs):
    pieces, out, stage, sems = refs[:ways], refs[-3], refs[-2], refs[-1]
    wide = pieces[0].shape[1]
    me = lax.axis_index("head")
    run_copies(
        [
            (pieces[r], out.at[:, pl.ds(column(me + r + turned(chunk), ways, width, start), wide)])
            for r in range(ways)
        ],
        stage,
        sems,
    )


def place(pieces, width, chunk, start, earlier):
    ways = len(pieces)
    rows = pieces[0].shape[0]
    extra = [] if earlier is None else [earlier]
    return pl.pallas_call(
        functools.partial(place_body, ways, width, chunk, start),
        out_shape=jax.ShapeDtypeStruct((rows, width), pieces[0].dtype),
        in_specs=[ANY] * (ways + len(extra)),
        out_specs=ANY,
        scratch_shapes=staging(ways, pieces[0].shape),
        input_output_aliases={ways: 0} if extra else {},
        compiler_params=pltpu.CompilerParams(vmem_limit_bytes=VMEM_LIMIT),
        cost_estimate=pl.CostEstimate(flops=BUSY, bytes_accessed=0, transcendentals=0),
        name="place",
    )(*pieces, *extra)


def turn(block, distance):
    if distance == 0:
        return block
    ways = lax.axis_size("head")
    return lax.ppermute(block, "head", [(i, (i + distance) % ways) for i in range(ways)])


def onward(block, chunk, relayed):
    count, ways = lax.axis_size("group"), lax.axis_size("head")
    half = count // 2
    pairs, last = [], []
    for group in range(count - 1):
        for i in range(ways):
            there = (group + 1) * ways + i
            if group + 1 == half:
                there = half * ways + (i - chunk[1]) % ways
                if relayed:
                    last.append((i, there))
                    there = i
            pairs.append((group * ways + i, there))
    block = lax.ppermute(block, ("group", "head"), pairs)
    if not relayed:
        return [block]
    return [block, lax.ppermute(block, ("group", "head"), last)]


def shards(queries, keys, values, noise_level, tile_mask):
    ways = lax.axis_size("head")
    width = queries.shape[1]
    order = (2, 1, 3, 0)
    packed = pack(queries, keys, values, ways, order)
    moved = [turn(block, order[i % ways]) for i, block in enumerate(packed)]
    parts = [
        [moved[i * ways + order.index(r)] for r in range(ways)] for i in range(1 + len(CHUNKS))
    ]
    pieces, asks = parts[:-1], parts[-1]
    gathered = []
    for part in pieces:
        gathered.append(gather(part, gathered[-1:]))
    priors = [
        onward(block, chunk, j < RELAYED) for j, (block, chunk) in enumerate(zip(gathered, CHUNKS))
    ]
    gates = [touch([prior[0] for prior in priors[RELAYED:]])]
    out = None
    for j, (chunk, start, _) in enumerate(spans()):
        result = attend(noise_level, tile_mask, pieces[j], asks, priors[j], chunk, start, gates)
        back = [result[0]] + [turn(result[r], ways - r) for r in range(1, ways)]
        out = place(back, width, chunk, start, out)
    return out


def solution(mesh):
    split = P(("group", "head"), None)
    in_specs = (split, split, split, P(), P("group", None, None))
    return jax.shard_map(shards, mesh=mesh, in_specs=in_specs, out_specs=split, check_vma=False)
```
